32 devices in a mesh: tok: 8 (over z, y), wid: 4 (over x, core).
Axes of the slice: x: 2, y: 2, z: 4, core: 2. Of those that a mesh axis runs over, the one named last changes fastest.
Arguments:
- g_inverse: bfloat16 [16384, 16384], P('tok', 'wid'), may hold values from -1 to 18, as said below
- a_inverse: bfloat16 [16384, 16384], P('tok', 'wid'), may hold values from -1 to 18, as said below
- query_out: bfloat16 [16384, 128], P(('tok', 'wid')), may hold values from -0.046875 to 0.046875
- query_in: bfloat16 [16384, 128], P(('tok', 'wid')), may hold values from -0.01171875 to 0.01171875
- output_grads: bfloat16 [16384, 16384], P('tok', 'wid'), may hold values from -6 to 6
- activations: bfloat16 [16384, 16384], P('tok', 'wid'), may hold values from -6 to 6
Outputs:
- scores: float32 [8, 16384], P(None, ('tok', 'wid'))
The draws below stay inside these ranges and needn't reach their ends.
Inputs may be any that keep to these rules, and one draw needn't show every extreme that they name: g_inverse is symmetric. a_inverse is symmetric.
All inputs are finite; a program needn't handle non-finite values.
Results may differ from the reference program's by a relative error of at most 0.0041.
Values may be sent and summed in bfloat16 or wider, within the bound.
No kernel may reach another device: no remote copies, remote signals or barrier semaphores. Data moves between devices by JAX's collectives and lax.ppermute only.
A program may use at most 128 MiB of HBM per device.

```python
import math
import jax
import jax.numpy as jnp

D = 16384
QUERIES = 8
RANK = 16
TOKENS = 16384


def kron_inverse(key, salt):
    key = jax.random.fold_in(key, salt)
    first, second = jax.random.split(key, 2)
    noise = jax.random.normal(first, (D, D), jnp.float32)
    matrix = (noise + noise.T) * (0.4 / math.sqrt(2.0 * D))
    diag_vals = jax.random.uniform(second, (D,), jnp.float32, 1.0, 2.0)
    matrix = matrix + jnp.diag(diag_vals)
    return matrix


def draw_g_inverse(key, part):
    return kron_inverse(key, 11).astype(jnp.bfloat16)


def draw_a_inverse(key, part):
    return kron_inverse(key, 23).astype(jnp.bfloat16)


def steps_of(key, shape, cuts, least, top_value):
    def one(axis_at, parts):
        steps = jax.random.uniform(jax.random.fold_in(jax.random.fold_in(key, 6), axis_at), (parts,), jnp.float32, least / len(cuts), top_value / len(cuts))
        return jnp.repeat(jnp.exp(steps), shape[axis_at] // parts).reshape((-1,) + (1,) * (len(shape) - axis_at - 1))

    level = one(*cuts[0])
    for cut in cuts[1:]:
        level = level * one(*cut)
    return level


def scatter_about(stream_key, shape, width, most, cuts=(), dtype=jnp.bfloat16):
    array = width * jax.random.normal(stream_key, shape, jnp.float32)
    if cuts:
        array = array * steps_of(stream_key, shape, cuts, -0.22, 0.18)
    return jnp.clip(array, -most, most).astype(dtype)


def setup_inputs(seed: int = 0) -> dict:
    key_of = jax.random.split(jax.random.key(seed), 7)
    return {
        "g_inverse": draw_g_inverse(jax.random.fold_in(key_of[6], 71), 0),
        "a_inverse": draw_a_inverse(jax.random.fold_in(key_of[6], 71), 0),
        "query_out": scatter_about(key_of[2], (D, QUERIES * RANK), D ** -0.5, 0.046875, ((0, 32),)),
        "query_in": scatter_about(key_of[3], (D, QUERIES * RANK), (D * RANK) ** -0.5, 0.01171875, ((0, 32),)),
        "output_grads": scatter_about(key_of[4], (TOKENS, D), 1.0, 6.0, ((0, 8), (1, 4))),
        "activations": scatter_about(key_of[5], (TOKENS, D), 1.0, 6.0, ((0, 8), (1, 4))),
    }


def reference(g_inverse, a_inverse, query_out, query_in, output_grads, activations):
    g_pre = jnp.dot(g_inverse, query_out, preferred_element_type=jnp.float32).astype(jnp.bfloat16)
    a_pre = jnp.dot(a_inverse, query_in, preferred_element_type=jnp.float32).astype(jnp.bfloat16)
    out_proj = jnp.dot(output_grads, g_pre, preferred_element_type=jnp.float32)
    in_proj = jnp.dot(activations, a_pre, preferred_element_type=jnp.float32)
    product = (out_proj * in_proj).reshape(TOKENS, QUERIES, RANK)
    return jnp.sum(product, axis=2).T
```

```python
import functools

import jax
import jax.numpy as jnp
import numpy as np
from jax import lax
from jax.experimental import pallas as pl
from jax.experimental.pallas import tpu as pltpu
from jax.sharding import PartitionSpec as P

QUERIES = 8
RANK = 16
LANES = 128
F32 = jnp.float32
BF16 = jnp.bfloat16
GRANT = 4 << 20
COST = 2
VMEM = pl.BlockSpec(memory_space=pltpu.VMEM)
SMEM = pl.BlockSpec(memory_space=pltpu.SMEM)
HBM = pl.BlockSpec(memory_space=pltpu.HBM)
WIRE_G = F32
WIRE_A = BF16
HOLD = 30 * 10**6
ANY = pl.BlockSpec(memory_space=pl.ANY)


def ring_order(size):
    rows = 1
    while rows * rows < size:
        rows *= 2
    cols = size // rows
    if rows * cols != size or cols < 2:
        return list(range(size))
    cycle = [(r, 0) for r in range(rows)]
    for i, r in enumerate(reversed(range(rows))):
        walk = range(1, cols) if i % 2 == 0 else range(cols - 1, 0, -1)
        cycle += [(r, c) for c in walk]
    return [r * cols + c for r, c in cycle]


def reversed_bits(j, bits):
    return sum(((j >> b) & 1) << (bits - 1 - b) for b in range(bits))


def gate_body(small, *refs):
    refs[-1][...] = small[...]


def gate(small, cost, after=()):
    return pl.pallas_call(
        gate_body,
        in_specs=[VMEM] + [ANY] * len(after),
        out_specs=VMEM,
        out_shape=jax.ShapeDtypeStruct(small.shape, small.dtype),
        compiler_params=pltpu.CompilerParams(vmem_limit_bytes=GRANT),
        cost_estimate=pl.CostEstimate(flops=0, bytes_accessed=cost, transcendentals=0),
    )(small, *after)


def turn_body(base, ids, *refs):
    queries, out = refs[:-1], refs[-1]
    height = queries[0].shape[0]
    for k, query in enumerate(queries):
        out[:, pl.ds(pl.multiple_of(ids[base + k] * height, height), height)] = query[...].T


def turn(ids, base, queries):
    return pl.pallas_call(
        functools.partial(turn_body, base),
        in_specs=[SMEM] + [VMEM] * len(queries),
        out_specs=VMEM,
        out_shape=jax.ShapeDtypeStruct((LANES, len(queries) * queries[0].shape[0]), BF16),
        compiler_params=pltpu.CompilerParams(vmem_limit_bytes=GRANT),
    )(ids, *queries)


def partials_body(columns, ids, turned, inverse, *refs):
    outs = refs[-len(columns) :]
    width = outs[0].shape[0]
    for column, out in zip(columns, outs):
        block = inverse[:, pl.ds(pl.multiple_of(ids[column] * width, width), width)]
        out[...] = jnp.dot(turned[...], block, preferred_element_type=F32).T


def partials(ids, turned, inverse, columns, width, after):
    n = len(columns)
    return pl.pallas_call(
        functools.partial(partials_body, columns),
        in_specs=[SMEM, VMEM, VMEM] + [ANY] * len(after),
        out_specs=[VMEM] * n,
        out_shape=[jax.ShapeDtypeStruct((width, LANES), F32)] * n,
        compiler_params=pltpu.CompilerParams(vmem_limit_bytes=GRANT),
        cost_estimate=pl.CostEstimate(
            flops=2 * n * width * turned.size,
            bytes_accessed=COST * n * width * inverse.shape[0],
            transcendentals=0,
        ),
    )(ids, turned, inverse, *after)


def project_body(columns, first, tile, count, ids, *refs):
    n, tokens, out = len(columns), refs[-2], refs[-1]
    factors, total = refs[:n], None if first else refs[n]
    height = tokens.shape[0] // count
    for j in range(count):
        rows = slice(j * height, (j + 1) * height)
        here = pl.ds(pl.multiple_of(ids[tile + j] * height, height), height)
        acc = None if first else total[rows, :]
        for column, factor in zip(columns, factors):
            width = factor.shape[0]
            block = tokens[here, pl.ds(pl.multiple_of(ids[column] * width, width), width)]
            term = jnp.dot(block, factor[...], preferred_element_type=F32)
            acc = term if acc is None else acc + term
        out[rows, :] = acc


def project(ids, columns, factors, total, tokens, tile, count):
    n, first = len(factors), total is None
    rows, width = tokens.shape[0], factors[0].shape[0]
    return pl.pallas_call(
        functools.partial(project_body, columns, first, tile, count),
        in_specs=[SMEM] + [VMEM] * (n + (not first) + 1),
        out_specs=VMEM,
        out_shape=jax.ShapeDtypeStruct((rows, LANES), F32),
        compiler_params=pltpu.CompilerParams(vmem_limit_bytes=GRANT),
        cost_estimate=pl.CostEstimate(
            flops=2 * n * rows * width * LANES,
            bytes_accessed=COST * n * rows * width,
            transcendentals=0,
        ),
    )(ids, *factors, *([] if first else [total]), tokens)


def score_body(out_ref, in_ref, arrived_ref, scores_ref):
    product = out_ref[...] * (in_ref[...] + arrived_ref[...].astype(F32))
    scores_ref[...] = product.T.reshape(QUERIES, RANK, product.shape[0]).sum(axis=1)


def score(out_proj, in_proj, arrived):
    rows = out_proj.shape[0]
    return pl.pallas_call(score_body, out_shape=jax.ShapeDtypeStruct((QUERIES, rows), F32))(
        out_proj, in_proj, arrived
    )


def program(tok, wid, g_inverse, a_inverse, query_out, query_in, output_grads, activations):
    bits = wid.bit_length() - 1
    cycle = ring_order(tok)
    width = g_inverse.shape[1] // tok
    height = g_inverse.shape[0] // wid
    share = output_grads.shape[0] // wid
    ahead, behind = tok // 2, (tok - 1) // 2
    sides = max(ahead, behind + 1)
    kernels = width % LANES == 0 and height % LANES == 0 and share % LANES == 0

    row_at, tile_at = tok, tok + wid
    table = np.zeros((tok, wid, tok + 2 * wid), np.int32)
    for t in range(tok):
        for w in range(wid):
            table[t, w, :tok] = (cycle.index(t) + np.arange(tok)) % tok
            table[t, w, row_at:tile_at] = w ^ np.arange(wid)
            table[t, w, tile_at:] = [w ^ reversed_bits(j, bits) for j in range(wid)]
    ids = jnp.asarray(table)[lax.axis_index("tok"), lax.axis_index("wid")]

    def shift(x, step):
        return lax.ppermute(x, "tok", [(cycle[i], cycle[(i + step) % tok]) for i in range(tok)])

    def swap(x, mask):
        return lax.ppermute(x, "wid", [(w, w ^ mask) for w in range(wid)])

    def at(offset):
        return offset % tok

    def gather_query(query):
        return [query] + [swap(query, k) for k in range(1, wid)]

    def make_partials(inverse, queries, columns):
        outs = []
        for column in columns:
            cut = lax.dynamic_slice_in_dim(inverse, ids[column] * width, width, 1)
            total = 0
            for k, query in enumerate(queries):
                block = lax.dynamic_slice_in_dim(cut, ids[row_at + k] * height, height, 0)
                total += lax.dot_general(block, query, (((0,), (0,)), ((), ())), preferred_element_type=F32)
            outs.append(total)
        return outs

    def make_project(tokens, columns, factors, total):
        outs = []
        for j in range(wid):
            cut = lax.dynamic_slice_in_dim(tokens, ids[tile_at + j] * share, share, 0)
            part = 0 if total is None else total[j * share : (j + 1) * share]
            for factor, column in zip(factors, columns):
                block = lax.dynamic_slice_in_dim(cut, ids[column] * width, width, 1)
                part += jnp.dot(block, factor, preferred_element_type=F32)
            outs.append(part)
        return jnp.concatenate(outs, axis=0)

    def precondition(inverse, queries, way, wire, after):
        turned = turn(ids, row_at, queries) if kernels else queries
        first = None
        for k in range(sides + 1):
            if k == 1:
                front, back = fwd.astype(wire), bwd.astype(wire)
            if 1 <= k <= ahead:
                last, front = front, shift(front, way)
            if 1 <= k <= behind:
                back = shift(back, -way)
            if k < sides:
                columns = [at(way * (ahead - k)), at(way * (k - behind))]
                if kernels:
                    fwd, bwd = partials(ids, turned, inverse, columns, width, after if k == 0 else [last])
                else:
                    fwd, bwd = make_partials(inverse, queries, columns)
                last = first = fwd if k == 0 else first
            if 1 <= k < ahead:
                front = (front.astype(F32) + fwd).astype(wire)
            if 1 <= k < behind:
                back = (back.astype(F32) + bwd).astype(wire)
        return (front.astype(F32) + back.astype(F32) + bwd).astype(BF16), first

    def gather_project(tokens, factor, way, cuts):
        front = back = factor
        total = None
        factors, columns = [factor], [at(0)]
        for k in range(1, ahead + 1):
            front = shift(front, way)
            factors.append(front)
            columns.append(at(-way * k))
            if k <= behind:
                back = shift(back, -way)
                factors.append(back)
                columns.append(at(way * k))
            if k in cuts or k == ahead:
                if kernels:
                    total = project(ids, columns, factors, total, tokens, tile_at, wid)
                else:
                    total = make_project(tokens, columns, factors, total)
                factors, columns = [], []
        return total

    def scatter(total, last):
        for b in range(bits):
            half = total.shape[0] // 2
            arrived = swap(total[half:], 1 << b)
            if b == bits - 1 and not last:
                return total[:half], arrived
            total = total[:half] + arrived
        return total

    q_in = gather_query(query_in)
    if kernels:
        query_out = gate(query_out, HOLD)
    q_out = gather_query(query_out)
    a_pre, first = precondition(a_inverse, q_in, 1, WIRE_A, [])
    g_pre, _ = precondition(g_inverse, q_out, -1, WIRE_G, [first])
    in_proj = scatter(gather_project(activations, a_pre, 1, ()), True)
    out_proj, arrived = scatter(gather_project(output_grads, g_pre, -1, (2,)), False)
    return score(in_proj, out_proj, arrived)


def solution(mesh):
    return jax.shard_map(
        functools.partial(program, mesh.shape["tok"], mesh.shape["wid"]),
        mesh=mesh,
        in_specs=(
            P("tok", "wid"),
            P("tok", "wid"),
            P(("tok", "wid"), None),
            P(("tok", "wid"), None),
            P("tok", "wid"),
            P("tok", "wid"),
        ),
        out_specs=P(None, ("tok", "wid")),
        check_vma=False,
    )
```

```python
import functools

import jax
import jax.numpy as jnp
import numpy as np
from jax import lax
from jax.experimental import pallas as pl
from jax.experimental.pallas import tpu as pltpu
from jax.sharding import PartitionSpec as P

QUERIES = 8
RANK = 16
LANES = 128
F32 = jnp.float32
BF16 = jnp.bfloat16
GRANT = 4 << 20
COST = 2
VMEM = pl.BlockSpec(memory_space=pltpu.VMEM)
SMEM = pl.BlockSpec(memory_space=pltpu.SMEM)
HBM = pl.BlockSpec(memory_space=pltpu.HBM)
EARLY = 1 << 10
LATE = 6 << 20
MARKS_A = {}
MARKS_G = {1: 24 << 20, 2: 24 << 20}
ANY = pl.BlockSpec(memory_space=pl.ANY)


def ring_order(size):
    rows = 1
    while rows * rows < size:
        rows *= 2
    cols = size // rows
    if rows * cols != size or cols < 2:
        return list(range(size))
    cycle = [(r, 0) for r in range(rows)]
    for i, r in enumerate(reversed(range(rows))):
        walk = range(1, cols) if i % 2 == 0 else range(cols - 1, 0, -1)
        cycle += [(r, c) for c in walk]
    return [r * cols + c for r, c in cycle]


def hbm(x):
    return pltpu.with_memory_space_constraint(x, pltpu.HBM)


def reversed_bits(j, bits):
    return sum(((j >> b) & 1) << (bits - 1 - b) for b in range(bits))


def partials_body(n, row, step, begin, more, along, ids, *refs):
    queries, refs = refs[:n], refs[n:]
    if more:
        sums, refs = refs[0], refs[1:]
    if along:
        (small, inverse, outs, small_out), refs = refs[:4], refs[4:]
    else:
        (inverse, outs), refs = refs[:2], refs[2:]
    held, arrived = refs
    height, (count, width) = queries[0].shape[0], outs.shape[:2]
    copies = []
    for b in range(count):
        columns = pl.ds(pl.multiple_of(ids[step + begin + b] * width, width), width)
        for k in range(n):
            rows = pl.ds(pl.multiple_of(ids[row + k] * height, height), height)
            copy = pltpu.make_async_copy(inverse.at[rows, columns], held.at[b, pl.ds(k * height, height), :], arrived.at[b, k])
            copy.start()
            copies.append(copy)
    if along:
        small_out[...] = small[...]
    turned = jnp.concatenate([query[...].T for query in queries], axis=1)
    for b in range(count):
        for copy in copies[b * n : (b + 1) * n]:
            copy.wait()
        part = jnp.dot(turned, held[b], preferred_element_type=F32).T
        outs[b] = part + sums[begin + b] if more else part


def partials(ids, inverse, queries, row, step, begin, count, width, sums=None, along=None, cost=1024):
    n, height, more = len(queries), queries[0].shape[0], sums is not None
    extra = [] if along is None else [along]
    shapes = [jax.ShapeDtypeStruct((count, width, LANES), F32)] + [jax.ShapeDtypeStruct(x.shape, x.dtype) for x in extra]
    return pl.pallas_call(
        functools.partial(partials_body, n, row, step, begin, more, along is not None),
        in_specs=[SMEM] + [VMEM] * (n + more + len(extra)) + [HBM],
        out_specs=[VMEM] * len(shapes),
        out_shape=shapes,
        scratch_shapes=[
            pltpu.VMEM((count, n * height, width), BF16),
            pltpu.SemaphoreType.DMA((count, n)),
        ],
        compiler_params=pltpu.CompilerParams(vmem_limit_bytes=2 * n * height * count * width + (6 << 20)),
        cost_estimate=pl.CostEstimate(flops=0, bytes_accessed=cost, transcendentals=0),
    )(ids, *queries, *([sums] if more else []), *extra, hbm(inverse))


def mark_body(small, out):
    out[...] = small[...]


def mark(small, cost):
    return pl.pallas_call(
        mark_body,
        in_specs=[VMEM],
        out_specs=VMEM,
        out_shape=jax.ShapeDtypeStruct(small.shape, small.dtype),
        compiler_params=pltpu.CompilerParams(vmem_limit_bytes=GRANT),
        cost_estimate=pl.CostEstimate(flops=0, bytes_accessed=cost, transcendentals=0),
    )(small)


def project_body(columns, first, tile, count, ids, *refs):
    n, (out, tick) = len(columns), refs[-2:]
    tick[...] = jnp.zeros_like(tick)
    factors, total = refs[:n], None if first else refs[n]
    tokens = refs[n + (not first)]
    height = tokens.shape[0] // count
    for j in range(count):
        rows = slice(j * height, (j + 1) * height)
        here = pl.ds(pl.multiple_of(ids[tile + j] * height, height), height)
        acc = None if first else total[rows, :]
        for column, factor in zip(columns, factors):
            width = factor.shape[0]
            block = tokens[here, pl.ds(pl.multiple_of(ids[column] * width, width), width)]
            term = jnp.dot(block, factor[...], preferred_element_type=F32)
            acc = term if acc is None else acc + term
        out[rows, :] = acc


def project(ids, columns, factors, total, tokens, tile, count, waits=()):
    n, first = len(factors), total is None
    rows, width = tokens.shape[0], factors[0].shape[0]
    return pl.pallas_call(
        functools.partial(project_body, columns, first, tile, count),
        in_specs=[SMEM] + [VMEM] * (n + (not first) + 1) + [ANY] * len(waits),
        out_specs=[VMEM, VMEM],
        out_shape=[jax.ShapeDtypeStruct((rows, LANES), F32), jax.ShapeDtypeStruct((8, LANES), F32)],
        compiler_params=pltpu.CompilerParams(vmem_limit_bytes=GRANT),
        cost_estimate=pl.CostEstimate(
            flops=2 * n * rows * width * LANES,
            bytes_accessed=COST * n * rows * width,
            transcendentals=0,
        ),
    )(ids, *factors, *([] if first else [total]), tokens, *waits)


def score_body(out_ref, in_ref, arrived_ref, scores_ref):
    product = out_ref[...] * (in_ref[...] + arrived_ref[...].astype(F32))
    scores_ref[...] = product.T.reshape(QUERIES, RANK, product.shape[0]).sum(axis=1)


def score(out_proj, in_proj, arrived):
    rows = out_proj.shape[0]
    return pl.pallas_call(
        score_body,
        in_specs=[VMEM] * 3,
        out_specs=VMEM,
        out_shape=jax.ShapeDtypeStruct((QUERIES, rows), F32),
    )(
        out_proj, in_proj, arrived
    )


def program(tok, wid, g_inverse, a_inverse, query_out, query_in, output_grads, activations):
    bits = wid.bit_length() - 1
    cycle = ring_order(tok)
    width = g_inverse.shape[1] // tok
    height = g_inverse.shape[0] // wid
    share = output_grads.shape[0] // wid
    ahead, behind = tok // 2, (tok - 1) // 2
    sides = max(ahead, behind + 1)
    kernels = width % LANES == 0 and height % LANES == 0 and share % LANES == 0

    row_at, tile_at, step_at = tok, tok + wid, tok + 2 * wid
    table = np.zeros((tok, wid, 3 * tok + 2 * wid), np.int32)
    order = {way: [way * o % tok for k in range(tok // 2) for o in (tok // 2 - k, k - (tok - 1) // 2)] for way in (1, -1)}
    for t in range(tok):
        for w in range(wid):
            table[t, w, :tok] = (cycle.index(t) + np.arange(tok)) % tok
            table[t, w, row_at:tile_at] = w ^ np.arange(wid)
            table[t, w, tile_at:step_at] = [w ^ reversed_bits(j, bits) for j in range(wid)]
            table[t, w, step_at:] = table[t, w, order[1] + order[-1]]
    ids = jnp.asarray(table)[lax.axis_index("tok"), lax.axis_index("wid")]

    def shift(x, step):
        return lax.ppermute(x, "tok", [(cycle[i], cycle[(i + step) % tok]) for i in range(tok)])

    def swap(x, mask):
        return lax.ppermute(x, "wid", [(w, w ^ mask) for w in range(wid)])

    def at(offset):
        return offset % tok

    def gather_query(query):
        return [query] + [swap(query, k) for k in range(1, wid)]

    def make_partials(inverse, queries, columns):
        outs = []
        for column in columns:
            cut = lax.dynamic_slice_in_dim(inverse, ids[column] * width, width, 1)
            total = 0
            for k, query in enumerate(queries):
                block = lax.dynamic_slice_in_dim(cut, ids[row_at + k] * height, height, 0)
                total += lax.dot_general(block, query, (((0,), (0,)), ((), ())), preferred_element_type=F32)
            outs.append(total)
        return outs

    def make_project(tokens, columns, factors, total):
        outs = []
        for j in range(wid):
            cut = lax.dynamic_slice_in_dim(tokens, ids[tile_at + j] * share, share, 0)
            part = 0 if total is None else total[j * share : (j + 1) * share]
            for factor, column in zip(factors, columns):
                block = lax.dynamic_slice_in_dim(cut, ids[column] * width, width, 1)
                part += jnp.dot(block, factor, preferred_element_type=F32)
            outs.append(part)
        return jnp.concatenate(outs, axis=0)

    def end_partials(inverse, queries, sums, way, cost):
        half, step = 0 if sums is None else wid // 2, step_at + (tok if way < 0 else 0)
        (one,) = partials(ids, inverse, queries[half:], row_at + half, step, 0, 2, width, sums, cost=cost)
        (two,) = partials(ids, inverse, queries[half:], row_at + half, step, 2, tok - 2, width, sums, cost=cost)
        return [one[0], one[1]] + [two[i] for i in range(tok - 2)]

    def precondition(terms, way, narrow, marks):
        fwd, bwd = terms[0::2], terms[1::2]
        front, back = fwd[0], bwd[0]
        for k in range(1, sides + 1):
            if k <= ahead:
                front = shift(front.astype(BF16 if k <= narrow else F32), way).astype(F32)
            if k <= behind:
                back = shift(back.astype(BF16 if k < narrow or narrow >= ahead else F32), -way).astype(F32)
            if k < ahead:
                front = front + fwd[k]
                if k in marks and kernels:
                    front = mark(front, marks[k])
            if k < behind:
                back = back + bwd[k]
        return (front + back + bwd[behind]).astype(BF16)

    def gather_project(tokens, factor, way, tied=True, waits=()):
        front = back = factor
        total = tick = None
        factors, columns = [factor], [at(0)]
        for k in range(1, ahead + 1):
            if tick is not None and tied:
                front = (front.astype(F32) + tick[:1]).astype(BF16)
                tick = None
            front = shift(front, way)
            if k <= behind:
                back = shift(back, -way)
            if k == ahead - 1 and kernels:
                total, tick = project(ids, columns, factors, total, tokens, tile_at, wid)
                factors, columns = [], []
            factors.append(front)
            columns.append(at(-way * k))
            if k <= behind:
                factors.append(back)
                columns.append(at(way * k))
        if kernels:
            return project(ids, columns, factors, total, tokens, tile_at, wid, waits)[0]
        return make_project(tokens, columns, factors, total)

    def scatter(total, last):
        for b in range(bits):
            half = total.shape[0] // 2
            arrived = swap(total[half:], 1 << b)
            if b == bits - 1 and not last:
                return total[:half], arrived
            total = total[:half] + arrived
        return total

    half = wid // 2
    q_in = gather_query(query_in)
    if kernels:
        a_half, query_out = partials(ids, a_inverse, q_in[:half], row_at, step_at, 0, tok, width, along=query_out)
        q_out = gather_query(query_out)
        a_terms = end_partials(a_inverse, q_in, a_half, 1, EARLY)
        g_terms = end_partials(g_inverse, q_out, None, -1, LATE)
    else:
        q_out = gather_query(query_out)
        a_terms = make_partials(a_inverse, q_in, order[1])
        g_terms = make_partials(g_inverse, q_out, order[-1])
    a_pre = precondition(a_terms, 1, ahead, MARKS_A)
    g_pre = precondition(g_terms, -1, ahead // 2, MARKS_G)
    in_proj = scatter(gather_project(activations, a_pre, 1), True)
    out_proj, arrived = scatter(gather_project(output_grads, g_pre, -1), False)
    return score(in_proj, out_proj, arrived)


def solution(mesh):
    return jax.shard_map(
        functools.partial(program, mesh.shape["tok"], mesh.shape["wid"]),
        mesh=mesh,
        in_specs=(
            P("tok", "wid"),
            P("tok", "wid"),
            P(("tok", "wid"), None),
            P(("tok", "wid"), None),
            P("tok", "wid"),
            P("tok", "wid"),
        ),
        out_specs=P(None, ("tok", "wid")),
        check_vma=False,
    )
```
